32 devices in a mesh: groups: 2 (over y), width: 4 (over z), hidden: 4 (over x, core).
Axes of the slice: x: 2, y: 2, z: 4, core: 2. Of those that a mesh axis runs over, the one named last changes fastest.
Arguments:
- tokens: bfloat16 [1024, 6144], P(('groups', 'hidden'), 'width'), parts along dimension 0, may hold values from -6 to 6
- expert_ids: int32 [1024, 2], P(('groups', 'hidden')), parts along dimension 0, may hold values from 0 to 7, all different within a row; in each aligned block of 128 rows (0 to 127, 128 to 255, ...) at most 64 rows name the same one
- skip_mask: int32 [1024], P(('groups', 'hidden')), parts along dimension 0, may hold values from 0 to 1, as said below
- pair_logits: float32 [1024, 2], P(('groups', 'hidden')), parts along dimension 0, may hold values from -6 to 8, as said below
- gate_up_weight: bfloat16 [2, 6144, 2, 16384], P(None, 'width', None, 'hidden'), may hold values from -0.078125 to 0.078125
- down_weight: bfloat16 [2, 16384, 6144], P(None, 'hidden', 'width'), may hold values from -0.046875 to 0.046875
Outputs:
- mixed: bfloat16 [1024, 6144], P(('groups', 'hidden'), 'width'), parts along dimension 0
The draws below stay inside these ranges and needn't reach their ends.
There are 2 independent parts, one for each index of `groups`. The reference program is written for one: setup_inputs(seed, part) draws one part's arguments, and reference() takes and returns one part's arrays. A program takes and returns all parts, laid end to end along the dimension named above; an argument that names none is the same for every part. Nothing has to cross between parts.
Inputs may be any that keep to these rules, and one draw needn't show every extreme that they name: `expert_ids`: each token names 2 different experts; among the tokens of one index of hidden no expert is named more than 64 times, a bound that some block reaches. skip_mask[t] is 1 exactly where second_weight[t] < 0.3 * first_weight[t]. For each token pair_logits[t, 0] >= pair_logits[t, 1].
All inputs are finite; a program needn't handle non-finite values.
Results may differ from the reference program's by a relative error of at most 0.02.
Values may be sent and summed in bfloat16 or wider, within the bound.
No kernel may reach another device: no remote copies, remote signals or barrier semaphores. Data moves between devices by JAX's collectives and lax.ppermute only.
A program may use at most 192 MiB of HBM per device.

```python
import math
import jax
import jax.numpy as jnp
import numpy as np
from jax import lax

D = 6144
FF = 16384
EXPERTS = 8
TOP = 2
EXP_WIN = 2
TOK_DEV = 128
TOKENS = 512
MOST_DEV = 64
N_WIDTH = 4
N_HIDDEN = 4


def skip_bits(key):
    mask_key = jax.random.fold_in(key, 11)
    return (jax.random.randint(mask_key, (TOKENS,), 0, 10) < 3).astype(jnp.int32)


def draw_skip_mask(key, part):
    bits = skip_bits(key)
    return bits


def draw_pair_logits(key, part):
    bits = skip_bits(key)
    key = jax.random.fold_in(key, 5)
    base_key, gap_key = jax.random.split(key)
    second = jnp.clip(1.5 * jax.random.normal(base_key, (TOKENS,), jnp.float32), -6.0, 3.0)
    unit = jax.random.uniform(gap_key, (TOKENS,), jnp.float32, 0.0, 1.0)
    gap = jnp.where(bits == 1, 1.4 + 3.6 * unit, unit)
    first = second + gap
    return jnp.stack([first, second], axis=1).astype(jnp.float32)


def block_scale(own_key, extent, cuts, smallest, top_value):
    level = 1.0
    for position, shards_of in cuts:
        heights = jax.random.uniform(jax.random.fold_in(jax.random.fold_in(own_key, 6), position), (shards_of,), jnp.float32, smallest / len(cuts), top_value / len(cuts))
        level = level * jnp.repeat(jnp.exp(heights), extent[position] // shards_of).reshape((-1,) + (1,) * (len(extent) - 1 - position))
    return level


def assign_block(key, own, number, rows, amount, top, reach, slope):
    order = jax.random.permutation(key, amount)
    heavy_load, usual = portions_of(amount, rows * top, reach, slope, True), portions_of(amount, rows * top, reach, slope, False)
    places = jnp.arange(amount)

    def named(tallies, rotation):
        used = int((tallies > 0).sum())
        fixed = max(1, used // 4)
        moved = fixed + (places - fixed + rotation * (used - fixed)) % max(1, amount - fixed)
        return jnp.zeros((amount,), jnp.int32).at[order[jnp.where(places < fixed, places, moved)]].set(jnp.asarray(tallies, jnp.int32))

    tallies = jnp.where(number % 4 == 0, named(heavy_load, number // 4), named(usual, number - number // 4 - 1))
    mixed = jax.random.permutation(jax.random.fold_in(own, 3), amount)
    source_of, receiver = mixed[0:amount // 2 * 2:2], mixed[1:amount // 2 * 2:2]
    slack = jnp.minimum(tallies[source_of] - 1, reach - tallies[receiver]) // 2
    slack = jnp.where((source_of == order[0]) | (receiver == order[0]) | (tallies[receiver] == 0), 0, jnp.maximum(slack, 0))
    moved = jax.random.randint(jax.random.fold_in(own, 4), (amount // 2,), 0, 1 << 20) % (slack + 1)
    tallies = tallies.at[source_of].add(-moved).at[receiver].add(moved)
    labels = jnp.searchsorted(jnp.cumsum(tallies), jnp.arange(rows * top), side="right").astype(jnp.int32)
    grid = labels.reshape(top, rows).T
    grid = grid[jax.random.permutation(jax.random.fold_in(own, 1), rows)]
    rotation = jax.random.randint(jax.random.fold_in(own, 2), (rows, 1), 0, top)
    return jnp.take_along_axis(grid, (jnp.arange(top)[None, :] + rotation) % top, axis=1)


def portions_of(count, total, reach, skew, full):
    weights = [(1 << 20) // math.isqrt(rank ** skew) + 1 for rank in range(1, count + 1)]
    largest = reach if full else min(reach, max(-(-total // count), total * weights[0] // sum(weights)))
    least = 1 if total - largest >= count - 1 else 0
    holding, spare = [largest] + [least] * (count - 1), total - largest - least * (count - 1)
    while spare > 0:
        candidates = [i for i in range(1, count) if holding[i] < largest] or [i for i in range(1, count) if holding[i] < reach]
        whole, budget = sum([weights[i] for i in candidates]), spare
        for i in candidates:
            more = min(reach - holding[i], max(1, budget * weights[i] // whole), spare)
            holding[i] = holding[i] + more
            spare = spare - more
    return np.array(holding)


def bell_draw(rng, extent, spread, bound, cuts=(), held_as=jnp.bfloat16):
    loudness = block_scale(rng, extent, cuts, -0.22, 0.18) if cuts else 1.0
    drawn = jax.random.normal(rng, extent, jnp.float32) * spread * loudness
    return jnp.minimum(jnp.maximum(drawn, -bound), bound).astype(held_as)


def setup_inputs(seed: int = 0, part: int = 0) -> dict:
    keys = jax.random.split(jax.random.key(seed), 7)
    own_keys = jax.random.split(jax.random.fold_in(keys[6], part), 7)
    tokens = bell_draw(own_keys[0], (TOKENS, D), 1.0, 6.0, ((0, 4), (1, 4)))
    expert_ids_keys = jax.random.split(jax.random.fold_in(own_keys[1], 1), TOKENS // TOK_DEV)
    expert_ids_turns = jax.random.permutation(jax.random.fold_in(own_keys[1], 3), TOKENS // TOK_DEV)
    expert_ids = jax.vmap(lambda own, number: assign_block(jax.random.fold_in(own_keys[1], 2), own, number, TOK_DEV, EXPERTS, TOP, MOST_DEV, 2))(expert_ids_keys, expert_ids_turns).reshape((TOKENS, TOP))
    skip_mask = draw_skip_mask(jax.random.fold_in(jax.random.fold_in(keys[6], part), 71), part)
    pair_logits = draw_pair_logits(jax.random.fold_in(jax.random.fold_in(keys[6], part), 71), part)
    gate_up_weight = bell_draw(keys[4], (EXP_WIN, D, 2, FF), D ** -0.5, 0.078125, ((1, 4), (3, 4)))
    down_weight = bell_draw(keys[5], (EXP_WIN, FF, D), FF ** -0.5, 0.046875, ((1, 4), (2, 4)))
    return {"tokens": tokens, "expert_ids": expert_ids, "skip_mask": skip_mask, "pair_logits": pair_logits, "gate_up_weight": gate_up_weight, "down_weight": down_weight}


def reference(tokens, expert_ids, skip_mask, pair_logits, gate_up_weight, down_weight):
    first_weight = jax.nn.sigmoid(pair_logits[:, 0] - pair_logits[:, 1])
    second_weight = jax.nn.sigmoid(pair_logits[:, 1] - pair_logits[:, 0])
    keep_second = skip_mask == 0
    width_rows = D // N_WIDTH
    capacity = MOST_DEV * N_HIDDEN
    owners = (jnp.arange(TOKENS, dtype=jnp.int32) // TOK_DEV).astype(jnp.int32)
    mixed = jnp.zeros((TOKENS, D), jnp.float32)
    for expert in range(EXP_WIN):
        hit_first = expert_ids[:, 0] == expert
        hit_second = (expert_ids[:, 1] == expert) & keep_second
        is_live = hit_first | hit_second
        ranking = jnp.cumsum(is_live.astype(jnp.int32).reshape(N_HIDDEN, TOK_DEV), axis=1).reshape(TOKENS) - 1
        slot_index = jnp.where(is_live, owners * MOST_DEV + ranking, capacity).astype(jnp.int32)
        buffer = jnp.zeros((capacity + 1, D), jnp.bfloat16).at[slot_index].set(tokens)[:capacity]
        weights_in = gate_up_weight[expert].reshape(D, 2 * FF)

        def add_shard(running, shard_index):
            first_row = (shard_index * width_rows).astype(jnp.int32)
            row_block = lax.dynamic_slice_in_dim(buffer, first_row, width_rows, 1).astype(jnp.float32)
            weight_block = lax.dynamic_slice_in_dim(weights_in, first_row, width_rows, 0).astype(jnp.float32)
            partial_value = jnp.dot(row_block, weight_block, preferred_element_type=jnp.float32)
            rounded = lax.optimization_barrier(partial_value.astype(jnp.bfloat16))
            return running + rounded.astype(jnp.float32), None

        both, _ = lax.scan(add_shard, jnp.zeros((capacity, 2 * FF), jnp.float32), jnp.arange(N_WIDTH, dtype=jnp.int32))
        both = both.reshape(capacity, 2, FF)
        hidden_rows = (jax.nn.silu(both[:, 0]) * both[:, 1]).astype(jnp.bfloat16)
        expert_out = jnp.dot(hidden_rows.astype(jnp.float32), down_weight[expert].astype(jnp.float32), preferred_element_type=jnp.float32)
        slot_scale = jnp.where(hit_first, first_weight, jnp.where(hit_second, second_weight, 0.0))
        picked = expert_out[jnp.minimum(slot_index, capacity - 1)]
        mixed = mixed + slot_scale[:, None] * picked
    return mixed.astype(jnp.bfloat16)
```

```python
import functools

import jax
import jax.numpy as jnp
import numpy as np
from jax import lax
from jax.experimental import pallas as pl
from jax.experimental.pallas import tpu as pltpu
from jax.sharding import PartitionSpec as P

MOST_DEV = 64
ROW = 16
FLAGS = 128
VMEM_LIMIT = 30 << 20
bf16, f32, i32 = jnp.bfloat16, jnp.float32, jnp.int32


def up_to(value, unit):
    return (value + unit - 1) // unit * unit


def pack_kernel(sel_ref, tok_ref, spread_ref, out_ref):
    experts, tiles, twice, _ = out_ref.shape
    tile = twice // 2
    cap = tiles * tile
    for e in range(experts):
        rows = jnp.dot(sel_ref[e], tok_ref[...], preferred_element_type=f32).astype(bf16)
        for g in range(2):
            wide = jnp.dot(rows, spread_ref[g], preferred_element_type=f32).astype(bf16)
            for i in range(tiles):
                out_ref[e, i, g * tile:(g + 1) * tile] = wide[i * tile:(i + 1) * tile]


def up_kernel(experts, slots, live_ref, plan_ref, x_ref, w_ref, *refs):
    out_ref, weight = refs[-2:]
    s, e = pl.program_id(0), pl.program_id(1)
    tile = x_ref.shape[2] // 2

    @pl.when(plan_ref[live_ref[2 * experts], s] != 0)
    def _():
        weight[...] = w_ref[0].reshape(weight.shape)

        @pl.loop(0, pl.cdiv(live_ref[e], tile))
        def _(i):
            both = jnp.dot(x_ref[e, i], weight[...], preferred_element_type=f32)
            row = pl.multiple_of(live_ref[experts + e] + i * tile, ROW)
            out_ref[0, 0, pl.ds(row, tile)] = both[:tile].astype(bf16)
            out_ref[0, 1, pl.ds(row, tile)] = both[tile:].astype(bf16)


def down_kernel(experts, tile, count, has_acc, live_ref, plan_ref, *refs):
    h_refs = refs[:count]
    w_ref = refs[count]
    acc_in = refs[count + 1] if has_acc else None
    acc, buf = refs[-2:]
    e, s = pl.program_id(0), pl.program_id(1)
    keep = h_refs[0].shape[0]

    @pl.when(s == 0)
    def _():
        acc[...] = acc_in[...] if has_acc else jnp.zeros_like(acc)

    @pl.when(plan_ref[live_ref[2 * experts], s] != 0)
    def _():
        for n in range(count):
            @pl.when(s == n)
            def _():
                buf[:keep] = h_refs[n][...]

        @pl.loop(0, pl.cdiv(live_ref[e], tile))
        def _(i):
            row = pl.multiple_of(live_ref[experts + e] + i * tile, ROW)
            acc[0, pl.ds(pl.multiple_of(i * tile, tile), tile)] += jnp.dot(
                buf[pl.ds(row, tile)], w_ref[0], preferred_element_type=f32
            )


def plan_rows(choices, experts, experts_inner):
    def row(z):
        blocks = [choice(z) for choice in choices]
        valid = [int(b is not None) for b in blocks]
        some = [b for b in blocks if b is not None]
        at = (0, some[0] if some else 0)
        steps = (
            [(s, e) for s in range(len(blocks)) for e in range(experts)]
            if experts_inner
            else [(s, e) for e in range(experts) for s in range(len(blocks))]
        )
        held = []
        for s, e in steps:
            if blocks[s] is not None:
                at = (e, blocks[s])
            held.append(at)
        return valid + [a for a, _ in held] + [b for _, b in held]
    return row


def up_call(x2, weight, live, plan, slots, keep, width, after):
    experts, tiles, twice, deep = x2.shape
    tile = twice // 2
    steps = slots * experts

    def w_index(s, e, live_ref, plan_ref):
        z, at = live_ref[2 * experts], slots + s * experts + e
        return plan_ref[z, at], 0, 0, plan_ref[z, at + steps]

    return pl.pallas_call(
        functools.partial(up_kernel, experts, slots),
        grid_spec=pltpu.PrefetchScalarGridSpec(
            num_scalar_prefetch=2,
            grid=(slots, experts),
            in_specs=[
                pl.BlockSpec(x2.shape, lambda *_: (0, 0, 0, 0), pipeline_mode=pl.Buffered(1)),
                pl.BlockSpec((1, deep // 2, 2, width), w_index),
            ] + [pl.BlockSpec(memory_space=pl.ANY)] * len(after),
            out_specs=pl.BlockSpec((1, 2, keep + tile, width), lambda s, e, *_: (s, 0, 0, 0)),
            scratch_shapes=[pltpu.VMEM((deep, width), bf16)],
        ),
        out_shape=jax.ShapeDtypeStruct((slots, 2, keep + tile, width), bf16),
        compiler_params=pltpu.CompilerParams(vmem_limit_bytes=VMEM_LIMIT),
        cost_estimate=pl.CostEstimate(
            flops=2 * steps * tiles * twice * deep * width,
            bytes_accessed=2 * steps * deep * width + 2 * x2.size,
            transcendentals=0,
        ),
    )(live, plan, x2, weight, *after)


def down_call(h_list, weight, live, plan, acc, cap, tile):
    experts, _, wide = weight.shape
    count = len(h_list)
    keep, fb = h_list[0].shape
    steps = count * experts

    def w_index(e, s, live_ref, plan_ref):
        z, at = live_ref[2 * experts], count + e * count + s
        return plan_ref[z, at], plan_ref[z, at + steps], 0

    acc_spec = pl.BlockSpec((1, cap, wide), lambda e, s, *_: (e, 0, 0))
    return pl.pallas_call(
        functools.partial(down_kernel, experts, tile, count, acc is not None),
        grid_spec=pltpu.PrefetchScalarGridSpec(
            num_scalar_prefetch=2,
            grid=(experts, count),
            in_specs=[pl.BlockSpec((keep, fb), lambda *_: (0, 0))] * count
            + [pl.BlockSpec((1, fb, wide), w_index)]
            + ([acc_spec] if acc is not None else []),
            out_specs=acc_spec,
            scratch_shapes=[pltpu.VMEM((experts * cap, fb), bf16)],
        ),
        out_shape=jax.ShapeDtypeStruct((experts, cap, wide), f32),
        compiler_params=pltpu.CompilerParams(vmem_limit_bytes=VMEM_LIMIT),
        cost_estimate=pl.CostEstimate(
            flops=2 * steps * cap * fb * wide,
            bytes_accessed=2 * steps * fb * wide + 8 * experts * cap * wide,
            transcendentals=0,
        ),
    )(live, plan, *h_list, weight, *([acc] if acc is not None else []))


def experts_on(keep, n, pieces, cap, tile, x2, live, weight_up, weight_down):
    experts = weight_up.shape[0]
    fb = weight_up.shape[-1] // n // pieces
    right = [(d, d + 1) for d in range(n - 1)]
    left = [(d + 1, d) for d in range(n - 1)]

    def plan_of(choices, experts_inner):
        row = plan_rows(choices, experts, experts_inner)
        return jnp.asarray(np.array([row(d) for d in range(n)], np.int32))

    def within(block, k, holds):
        return block * pieces + k if holds else None

    def shift(value, pairs):
        return lax.ppermute(value, "width", pairs)

    def to_right(k, t):
        return lambda d: within(d + n - 1 - t, k, d <= t and d < n - 1)

    def to_left(k, t):
        return lambda d: within(d - n + 1 + t, k, d >= n - 1 - t and d > 0)

    def at_home(k):
        return lambda d: within(d, k, True)

    def terms(k, first, last, home):
        choices = []
        for t in range(first, last):
            choices += [to_right(k, t), to_left(k, t)]
        choices += [at_home(k)] * home
        if not choices:
            return []
        out = up_call(x2, weight_up, live, plan_of(choices, True), len(choices), keep, fb, before)
        before[:] = [out]
        return [out[i, :, :keep] for i in range(len(choices))]

    def plus(got, term):
        return (got.astype(f32) + term.astype(f32)).astype(bf16)

    def down(held, choices, acc):
        if not held:
            return acc
        return down_call(held, weight_down, live, plan_of(choices, False), acc, cap, tile)

    acc = None
    before = []
    for k in range(pieces):
        if k == 0:
            part = terms(k, 0, 1, False) if n > 1 else []
            part += terms(k, 1, n - 1, True)
        else:
            part = terms(k, 0, n - 1, True)
        home = part[-1]
        got_r = got_l = None
        for t in range(n - 1):
            send_r, send_l = part[2 * t:2 * t + 2]
            if t:
                send_r, send_l = plus(got_r, send_r), plus(got_l, send_l)
            got_r = shift(send_r, [p for p in right if p[0] <= t])
            got_l = shift(send_l, [p for p in left if p[0] >= n - 1 - t])
        if acc is not None:
            home, acc = lax.optimization_barrier((home, acc))
        both = home.astype(f32)
        if n > 1:
            both = both + got_r.astype(f32) + got_l.astype(f32)
        hidden = (jax.nn.silu(both[0]) * both[1]).astype(bf16)
        held, choices = [hidden], [at_home(k)]
        go_r = go_l = hidden
        for t in range(n - 1):
            go_r = shift(go_r, [p for p in right if p[0] >= t])
            go_l = shift(go_l, [p for p in left if p[0] <= n - 1 - t])
            held += [go_r, go_l]
            choices += [
                lambda d, t=t, k=k: within(d - 1 - t, k, d - 1 - t >= 0),
                lambda d, t=t, k=k: within(d + 1 + t, k, d + 1 + t < n),
            ]
        cut = len(held) - 2 if k == pieces - 1 else len(held)
        acc = down(held[:cut], choices[:cut], acc)
        acc = down(held[cut:], choices[cut:], acc)
    return acc


def local(n_width, n_hidden, tokens, expert_ids, skip_mask, pair_logits, gate_up_weight, down_weight):
    experts = gate_up_weight.shape[0]
    rows, depth = tokens.shape
    cores = 2 if n_hidden % 2 == 0 else 1
    chips = n_hidden // cores
    cap = MOST_DEV * n_hidden
    tile = min(128, cap)
    total = rows * n_hidden

    first = jax.nn.sigmoid(pair_logits[:, 0] - pair_logits[:, 1])
    second = jax.nn.sigmoid(pair_logits[:, 1] - pair_logits[:, 0])
    lanes = []
    scales = []
    for e in range(experts):
        hit_first = expert_ids[:, 0] == e
        hit_second = (expert_ids[:, 1] == e) & (skip_mask == 0)
        lanes.append((hit_first | hit_second).astype(f32))
        scales.append(jnp.where(hit_first, first, jnp.where(hit_second, second, 0.0)))
    for scale in scales:
        for _ in range(3):
            part = lax.reduce_precision(scale, 8, 7)
            lanes.append(part)
            scale = scale - part
    flags = jnp.stack(lanes, axis=1)
    flags = jnp.pad(flags, ((0, 0), (0, FLAGS - flags.shape[1]))).astype(bf16)
    mine = jnp.concatenate([tokens, flags], axis=1)

    blocks = [mine]
    for dx in range(1, chips):
        blocks.append(lax.ppermute(mine, "hidden", [
            ((x + dx) % chips * cores + c, x * cores + c) for x in range(chips) for c in range(cores)
        ]))
    mine = jnp.concatenate(blocks, axis=0)
    swap = [(h, h ^ 1) for h in range(n_hidden)]
    if cores == 2:
        mine = jnp.concatenate([mine, lax.ppermute(mine, "hidden", swap)], axis=0)

    flags = mine[:, depth:].astype(f32)
    alive = flags[:, :experts]
    scale = flags[:, experts:4 * experts].reshape(total, experts, 3).sum(-1)
    tri = jnp.tril(jnp.ones((total, total), bf16))
    rank = jnp.dot(tri, alive.astype(bf16), preferred_element_type=f32).astype(i32) - 1
    slot = jnp.where(alive > 0, rank, -1)
    select = slot.T[:, None, :] == jnp.arange(cap, dtype=i32)[None, :, None]
    count = rank[-1] + 1
    offset = [jnp.zeros((), i32)]
    for e in range(experts):
        offset.append(offset[-1] + up_to(count[e], ROW))
    live = jnp.concatenate([count, jnp.stack([*offset[:-1], lax.axis_index("width")])])
    slot_scale = jnp.where(select, scale.T[:, None, :], 0.0).sum(-1)

    block = 256 if depth % 256 == 0 else 128
    spread = np.zeros((2, block, 2 * block), np.float32)
    for g in range(2):
        spread[g, np.arange(block), 2 * np.arange(block) + g] = 1
    picker = select.astype(bf16)
    x2 = pl.pallas_call(
        pack_kernel,
        grid=(depth // block,),
        in_specs=[
            pl.BlockSpec(picker.shape, lambda k: (0, 0, 0)),
            pl.BlockSpec((total, block), lambda k: (0, k)),
            pl.BlockSpec(spread.shape, lambda k: (0, 0, 0)),
        ],
        out_specs=pl.BlockSpec((experts, cap // tile, 2 * tile, 2 * block), lambda k: (0, 0, 0, k)),
        out_shape=jax.ShapeDtypeStruct((experts, cap // tile, 2 * tile, 2 * depth), bf16),
        compiler_params=pltpu.CompilerParams(vmem_limit_bytes=VMEM_LIMIT),
    )(picker, mine, jnp.asarray(spread, bf16))

    own_hidden = gate_up_weight.shape[-1] // n_width
    pieces = max(1, min(2, own_hidden // 128))
    most = experts * cap
    sizes = sorted({min(most, up_to(most * part // 16, ROW)) for part in (6, 8, 10, 12, 16)})
    run = [
        functools.partial(experts_on, keep, n_width, pieces, cap, tile) for keep in sizes
    ]
    need = offset[-2] + count[-1]
    which = sum((need > keep).astype(i32) for keep in sizes[:-1])
    out = lax.switch(which, run, x2, live, gate_up_weight, down_weight)

    used = jnp.arange(cap, dtype=i32)[None, :, None] < count[:, None, None]
    scaled = jnp.where(used, out * slot_scale[:, :, None], 0.0)
    high = lax.reduce_precision(scaled, 8, 7)
    low = (scaled - high).astype(bf16)
    term = functools.partial(jnp.einsum, "est,esd->td", preferred_element_type=f32)
    mixed = term(picker, high.astype(bf16)) + term(picker, low)
    if cores == 2:
        half = total // 2
        mixed = mixed[:half] + lax.ppermute(mixed[half:].astype(bf16), "hidden", swap).astype(f32)
    result = mixed[:rows]
    for dx in range(1, chips):
        piece = mixed[dx * rows:(dx + 1) * rows].astype(bf16)
        result = result + lax.ppermute(piece, "hidden", [
            (x * cores + c, (x + dx) % chips * cores + c) for x in range(chips) for c in range(cores)
        ]).astype(f32)
    return result.astype(bf16)


def solution(mesh):
    placed = (
        P(("groups", "hidden"), "width"),
        P(("groups", "hidden"), None),
        P(("groups", "hidden")),
        P(("groups", "hidden"), None),
        P(None, "width", None, "hidden"),
        P(None, "hidden", "width"),
    )
    return jax.shard_map(
        functools.partial(local, mesh.shape["width"], mesh.shape["hidden"]),
        mesh=mesh,
        in_specs=placed,
        out_specs=P(("groups", "hidden"), "width"),
        check_vma=False,
    )
```

```python
import functools

import jax
import jax.numpy as jnp
import numpy as np
from jax import lax
from jax.experimental import pallas as pl
from jax.experimental.pallas import tpu as pltpu
from jax.sharding import PartitionSpec as P

MOST_DEV = 64
ROW = 16
FLAGS = 128
VMEM_LIMIT = 30 << 20
bf16, f32, i32 = jnp.bfloat16, jnp.float32, jnp.int32


def up_to(value, unit):
    return (value + unit - 1) // unit * unit


def pack_kernel(sel_ref, tok_ref, spread_ref, out_ref):
    experts, tiles, twice, _ = out_ref.shape
    tile = twice // 2
    cap = tiles * tile
    for e in range(experts):
        rows = jnp.dot(sel_ref[e], tok_ref[...], preferred_element_type=f32).astype(bf16)
        for g in range(2):
            wide = jnp.dot(rows, spread_ref[g], preferred_element_type=f32).astype(bf16)
            for i in range(tiles):
                out_ref[e, i, g * tile:(g + 1) * tile] = wide[i * tile:(i + 1) * tile]


def up_kernel(experts, slots, live_ref, plan_ref, x_ref, w_ref, *refs):
    out_ref, weight = refs[-2:]
    s, e = pl.program_id(0), pl.program_id(1)
    tile = x_ref.shape[2] // 2

    @pl.when(plan_ref[live_ref[2 * experts], s] != 0)
    def _():
        weight[...] = w_ref[0].reshape(weight.shape)

        part = min(256, weight.shape[1])
        parts = weight.shape[1] // part

        @pl.loop(0, pl.cdiv(live_ref[e], tile) * parts)
        def _(n):
            i, j = n // parts, n % parts
            lanes = pl.ds(pl.multiple_of(j * part, part), part)
            both = jnp.dot(x_ref[e, i], weight[:, lanes], preferred_element_type=f32)
            row = pl.multiple_of(live_ref[experts + e] + i * tile, ROW)
            out_ref[0, 0, pl.ds(row, tile), lanes] = both[:tile].astype(bf16)
            out_ref[0, 1, pl.ds(row, tile), lanes] = both[tile:].astype(bf16)


def down_kernel(experts, count, has_acc, live_ref, plan_ref, *refs):
    h_refs = refs[:count]
    w_ref = refs[count]
    acc_in = refs[count + 1] if has_acc else None
    acc, buf = refs[-2:]
    e, s = pl.program_id(0), pl.program_id(1)
    keep = h_refs[0].shape[0]

    @pl.when(s == 0)
    def _():
        acc[...] = acc_in[...] if has_acc else jnp.zeros_like(acc)

    @pl.when(plan_ref[live_ref[2 * experts], s] != 0)
    def _():
        for n in range(count):
            @pl.when(s == n)
            def _():
                buf[:keep] = h_refs[n][...]
        row = pl.multiple_of(live_ref[experts + e], ROW)
        rows = buf[pl.ds(row, acc.shape[1])]
        part = min(512, acc.shape[2])

        @pl.loop(0, acc.shape[2] // part)
        def _(j):
            lanes = pl.ds(pl.multiple_of(j * part, part), part)
            acc[0, :, lanes] += jnp.dot(rows, w_ref[0, :, lanes], preferred_element_type=f32)


def plan_rows(choices, experts, experts_inner):
    def row(z):
        blocks = [choice(z) for choice in choices]
        valid = [int(b is not None) for b in blocks]
        some = [b for b in blocks if b is not None]
        at = (0, some[0] if some else 0)
        steps = (
            [(s, e) for s in range(len(blocks)) for e in range(experts)]
            if experts_inner
            else [(s, e) for e in range(experts) for s in range(len(blocks))]
        )
        held = []
        for s, e in steps:
            if blocks[s] is not None:
                at = (e, blocks[s])
            held.append(at)
        return valid + [a for a, _ in held] + [b for _, b in held]
    return row


def up_call(x2, weight, live, plan, slots, keep, width, after):
    experts, tiles, twice, deep = x2.shape
    tile = twice // 2
    steps = slots * experts

    def w_index(s, e, live_ref, plan_ref):
        z, at = live_ref[2 * experts], slots + s * experts + e
        return plan_ref[z, at], 0, 0, plan_ref[z, at + steps]

    return pl.pallas_call(
        functools.partial(up_kernel, experts, slots),
        grid_spec=pltpu.PrefetchScalarGridSpec(
            num_scalar_prefetch=2,
            grid=(slots, experts),
            in_specs=[
                pl.BlockSpec(x2.shape, lambda *_: (0, 0, 0, 0), pipeline_mode=pl.Buffered(1)),
                pl.BlockSpec((1, deep // 2, 2, width), w_index),
            ] + [pl.BlockSpec(memory_space=pl.ANY)] * len(after),
            out_specs=pl.BlockSpec((1, 2, keep + tile, width), lambda s, e, *_: (s, 0, 0, 0)),
            scratch_shapes=[pltpu.VMEM((deep, width), bf16)],
        ),
        out_shape=jax.ShapeDtypeStruct((slots, 2, keep + tile, width), bf16),
        compiler_params=pltpu.CompilerParams(vmem_limit_bytes=VMEM_LIMIT),
        cost_estimate=pl.CostEstimate(
            flops=2 * steps * tiles * twice * deep * width,
            bytes_accessed=2 * steps * deep * width + 2 * x2.size,
            transcendentals=0,
        ),
    )(live, plan, x2, weight, *after)


def down_call(h_list, weight, live, plan, acc, cap):
    experts, _, wide = weight.shape
    count = len(h_list)
    keep, fb = h_list[0].shape
    steps = count * experts

    def w_index(e, s, live_ref, plan_ref):
        z, at = live_ref[2 * experts], count + e * count + s
        return plan_ref[z, at], plan_ref[z, at + steps], 0

    acc_spec = pl.BlockSpec((1, cap, wide), lambda e, s, *_: (e, 0, 0))
    return pl.pallas_call(
        functools.partial(down_kernel, experts, count, acc is not None),
        grid_spec=pltpu.PrefetchScalarGridSpec(
            num_scalar_prefetch=2,
            grid=(experts, count),
            in_specs=[pl.BlockSpec((keep, fb), lambda *_: (0, 0))] * count
            + [pl.BlockSpec((1, fb, wide), w_index)]
            + ([acc_spec] if acc is not None else []),
            out_specs=acc_spec,
            scratch_shapes=[pltpu.VMEM((experts * cap, fb), bf16)],
        ),
        out_shape=jax.ShapeDtypeStruct((experts, cap, wide), f32),
        compiler_params=pltpu.CompilerParams(vmem_limit_bytes=VMEM_LIMIT),
        cost_estimate=pl.CostEstimate(
            flops=2 * steps * cap * fb * wide,
            bytes_accessed=2 * steps * fb * wide + 8 * experts * cap * wide,
            transcendentals=0,
        ),
    )(live, plan, *h_list, weight, *([acc] if acc is not None else []))


def experts_on(keep, n, pieces, cap, tile, x2, live, weight_up, weight_down):
    experts = weight_up.shape[0]
    fb = weight_up.shape[-1] // n // pieces
    right = [(d, d + 1) for d in range(n - 1)]
    left = [(d + 1, d) for d in range(n - 1)]

    def plan_of(choices, experts_inner):
        row = plan_rows(choices, experts, experts_inner)
        return jnp.asarray(np.array([row(d) for d in range(n)], np.int32))

    def within(block, k, holds):
        return block * pieces + k if holds else None

    def shift(value, pairs):
        return lax.ppermute(value, "width", pairs)

    def to_right(k, t):
        return lambda d: within(d + n - 1 - t, k, d <= t and d < n - 1)

    def to_left(k, t):
        return lambda d: within(d - n + 1 + t, k, d >= n - 1 - t and d > 0)

    def at_home(k):
        return lambda d: within(d, k, True)

    def terms(k, first, last, home, *after):
        choices = []
        for t in range(first, last):
            choices += [to_right(k, t), to_left(k, t)]
        choices += [at_home(k)] * home
        if not choices:
            return []
        out = up_call(x2, weight_up, live, plan_of(choices, True), len(choices), keep, fb, after)
        return [out[i, :, :keep] for i in range(len(choices))]

    def plus(got, term):
        return (got.astype(f32) + term.astype(f32)).astype(bf16)

    def down(held, choices, acc):
        if not held:
            return acc
        return down_call(held, weight_down, live, plan_of(choices, False), acc, cap)

    def send(k, t, part, got):
        right_sum, left_sum = part
        if t:
            right_sum, left_sum = plus(got[0], right_sum), plus(got[1], left_sum)
        sent[k, t] = right_sum
        return (
            shift(right_sum, [p for p in right if p[0] <= t]),
            shift(left_sum, [p for p in left if p[0] >= n - 1 - t]),
        )

    sent, got, parts = {}, {}, {}
    for k in range(pieces):
        follows = [sent[k - 1, min(1, n - 2)]] if k and n > 1 else []
        parts[k] = terms(k, 0, min(1, n - 1), False, *follows)
        if n > 1:
            got[k] = send(k, 0, parts[k], None)
            follows = [parts[k][0]]
            if k:
                follows.append(sent[k - 1, n - 2])
        parts[k] += terms(k, 1, n - 1, True, *follows)
        for t in range(1, n - 1):
            got[k] = send(k, t, parts[k][2 * t:2 * t + 2], got[k])

    acc = None
    late = []
    for k in range(pieces):
        home = parts[k][-1]
        if acc is not None:
            home, acc = lax.optimization_barrier((home, acc))
        both = home.astype(f32)
        if n > 1:
            both = both + got[k][0].astype(f32) + got[k][1].astype(f32)
        hidden = (jax.nn.silu(both[0]) * both[1]).astype(bf16)
        held, choices = [hidden], [at_home(k)]
        go_r = go_l = hidden
        for t in range(n - 1):
            if t == 1 and late:
                acc = down(*late.pop(), acc)
                go_r, acc = lax.optimization_barrier((go_r, acc))
            if t == 2:
                acc = down(held[:3], choices[:3], acc)
                if k == pieces - 1:
                    go_r, acc = lax.optimization_barrier((go_r, acc))
            go_r = shift(go_r, [p for p in right if p[0] >= t])
            go_l = shift(go_l, [p for p in left if p[0] <= n - 1 - t])
            held += [go_r, go_l]
            choices += [
                lambda d, t=t, k=k: within(d - 1 - t, k, d - 1 - t >= 0),
                lambda d, t=t, k=k: within(d + 1 + t, k, d + 1 + t < n),
            ]
        if n < 4:
            acc = down(held[:3], choices[:3], acc)
        late.append((held[3:], choices[3:]))
    for held, choices in late:
        for s in range(0, len(held), 2):
            acc = down(held[s:s + 2], choices[s:s + 2], acc)
    return acc


def local(n_width, n_hidden, tokens, expert_ids, skip_mask, pair_logits, gate_up_weight, down_weight):
    experts = gate_up_weight.shape[0]
    rows, depth = tokens.shape
    cores = 2 if n_hidden % 2 == 0 else 1
    chips = n_hidden // cores
    cap = MOST_DEV * n_hidden
    tile = min(128, cap)
    total = rows * n_hidden

    first = jax.nn.sigmoid(pair_logits[:, 0] - pair_logits[:, 1])
    second = jax.nn.sigmoid(pair_logits[:, 1] - pair_logits[:, 0])
    lanes = []
    scales = []
    for e in range(experts):
        hit_first = expert_ids[:, 0] == e
        hit_second = (expert_ids[:, 1] == e) & (skip_mask == 0)
        lanes.append((hit_first | hit_second).astype(f32))
        scales.append(jnp.where(hit_first, first, jnp.where(hit_second, second, 0.0)))
    for scale in scales:
        for _ in range(3):
            part = lax.reduce_precision(scale, 8, 7)
            lanes.append(part)
            scale = scale - part
    flags = jnp.stack(lanes, axis=1)
    flags = jnp.pad(flags, ((0, 0), (0, FLAGS - flags.shape[1]))).astype(bf16)

    swap = [(h, h ^ 1) for h in range(n_hidden)]

    def gather(value):
        blocks = [value]
        for dx in range(1, chips):
            blocks.append(lax.ppermute(value, "hidden", [
                ((x + dx) % chips * cores + c, x * cores + c)
                for x in range(chips) for c in range(cores)
            ]))
        value = jnp.concatenate(blocks, axis=0)
        if cores == 2:
            value = jnp.concatenate([value, lax.ppermute(value, "hidden", swap)], axis=0)
        return value

    flags = gather(flags).astype(f32)
    mine = gather(tokens)
    alive = flags[:, :experts]
    scale = flags[:, experts:4 * experts].reshape(total, experts, 3).sum(-1)
    tri = jnp.tril(jnp.ones((total, total), bf16))
    rank = jnp.dot(tri, alive.astype(bf16), preferred_element_type=f32).astype(i32) - 1
    slot = jnp.where(alive > 0, rank, -1)
    select = slot.T[:, None, :] == jnp.arange(cap, dtype=i32)[None, :, None]
    count = rank[-1] + 1
    offset = [jnp.zeros((), i32)]
    for e in range(experts):
        offset.append(offset[-1] + up_to(count[e], ROW))
    live = jnp.concatenate([count, jnp.stack([*offset[:-1], lax.axis_index("width")])])
    slot_scale = jnp.where(select, scale.T[:, None, :], 0.0).sum(-1)

    block = 256 if depth % 256 == 0 else 128
    spread = np.zeros((2, block, 2 * block), np.float32)
    for g in range(2):
        spread[g, np.arange(block), 2 * np.arange(block) + g] = 1
    picker = select.astype(bf16)
    x2 = pl.pallas_call(
        pack_kernel,
        grid=(depth // block,),
        in_specs=[
            pl.BlockSpec(picker.shape, lambda k: (0, 0, 0)),
            pl.BlockSpec((total, block), lambda k: (0, k)),
            pl.BlockSpec(spread.shape, lambda k: (0, 0, 0)),
        ],
        out_specs=pl.BlockSpec((experts, cap // tile, 2 * tile, 2 * block), lambda k: (0, 0, 0, k)),
        out_shape=jax.ShapeDtypeStruct((experts, cap // tile, 2 * tile, 2 * depth), bf16),
        compiler_params=pltpu.CompilerParams(vmem_limit_bytes=VMEM_LIMIT),
    )(picker, mine, jnp.asarray(spread, bf16))

    own_hidden = gate_up_weight.shape[-1] // n_width
    pieces = max(1, min(2, own_hidden // 128))
    most = experts * cap
    sizes = sorted({min(most, up_to(most * part // 32, ROW)) for part in (17, 21, 32)})
    run = [
        functools.partial(experts_on, keep, n_width, pieces, cap, tile) for keep in sizes
    ]
    need = offset[-2] + count[-1]
    which = sum((need > keep).astype(i32) for keep in sizes[:-1])
    out = lax.switch(which, run, x2, live, gate_up_weight, down_weight)

    used = jnp.arange(cap, dtype=i32)[None, :, None] < count[:, None, None]
    scaled = jnp.where(used, out * slot_scale[:, :, None], 0.0)
    high = lax.reduce_precision(scaled, 8, 7)
    low = (scaled - high).astype(bf16)
    term = functools.partial(jnp.einsum, "est,esd->td", preferred_element_type=f32)
    mixed = term(picker, high.astype(bf16)) + term(picker, low)
    if cores == 2:
        half = total // 2
        mixed = mixed[:half] + lax.ppermute(mixed[half:].astype(bf16), "hidden", swap).astype(f32)
    result = mixed[:rows]
    for dx in range(1, chips):
        piece = mixed[dx * rows:(dx + 1) * rows].astype(bf16)
        result = result + lax.ppermute(piece, "hidden", [
            (x * cores + c, (x + dx) % chips * cores + c) for x in range(chips) for c in range(cores)
        ]).astype(f32)
    return result.astype(bf16)


def solution(mesh):
    placed = (
        P(("groups", "hidden"), "width"),
        P(("groups", "hidden"), None),
        P(("groups", "hidden")),
        P(("groups", "hidden"), None),
        P(None, "width", None, "hidden"),
        P(None, "hidden", "width"),
    )
    return jax.shard_map(
        functools.partial(local, mesh.shape["width"], mesh.shape["hidden"]),
        mesh=mesh,
        in_specs=placed,
        out_specs=P(("groups", "hidden"), "width"),
        check_vma=False,
    )
```

```python
import functools

import jax
import jax.numpy as jnp
import numpy as np
from jax import lax
from jax.experimental import pallas as pl
from jax.experimental.pallas import tpu as pltpu
from jax.sharding import PartitionSpec as P

MOST_DEV = 64
ROW = 16
FLAGS = 128
VMEM_LIMIT = 30 << 20
bf16, f32, i32 = jnp.bfloat16, jnp.float32, jnp.int32


def up_to(value, unit):
    return (value + unit - 1) // unit * unit


def pack_kernel(sel_ref, tok_ref, spread_ref, out_ref):
    experts, tiles, twice, _ = out_ref.shape
    tile = twice // 2
    cap = tiles * tile
    for e in range(experts):
        rows = jnp.dot(sel_ref[e], tok_ref[...], preferred_element_type=f32).astype(bf16)
        for g in range(2):
            wide = jnp.dot(rows, spread_ref[g], preferred_element_type=f32).astype(bf16)
            for i in range(tiles):
                out_ref[e, i, g * tile:(g + 1) * tile] = wide[i * tile:(i + 1) * tile]


def up_kernel(experts, slots, live_ref, plan_ref, x_ref, w_ref, *refs):
    out_ref, weight = refs[-2:]
    s, e = pl.program_id(0), pl.program_id(1)
    tile = x_ref.shape[2] // 2

    @pl.when(plan_ref[live_ref[2 * experts], s] != 0)
    def _():
        step = 128

        @pl.loop(0, w_ref.shape[1] // step)
        def _(n):
            at = pl.multiple_of(n * step, step)
            weight[pl.ds(2 * at, 2 * step)] = w_ref[0, pl.ds(at, step)].reshape(2 * step, -1)

        part = min(256, weight.shape[1])
        parts = weight.shape[1] // part

        @pl.loop(0, pl.cdiv(live_ref[e], tile) * parts)
        def _(n):
            i, j = n // parts, n % parts
            lanes = pl.ds(pl.multiple_of(j * part, part), part)
            both = jnp.dot(x_ref[e, i], weight[:, lanes], preferred_element_type=f32)
            row = pl.multiple_of(live_ref[experts + e] + i * tile, ROW)
            out_ref[0, 0, pl.ds(row, tile), lanes] = both[:tile].astype(bf16)
            out_ref[0, 1, pl.ds(row, tile), lanes] = both[tile:].astype(bf16)


def down_kernel(experts, count, has_acc, live_ref, plan_ref, *refs):
    h_refs = refs[:count]
    w_ref = refs[count]
    acc_in = refs[count + 1] if has_acc else None
    acc, buf = refs[-2:]
    e, s = pl.program_id(0), pl.program_id(1)
    keep = h_refs[0].shape[0]

    @pl.when(s == 0)
    def _():
        acc[...] = acc_in[...] if has_acc else jnp.zeros_like(acc)

    @pl.when(plan_ref[live_ref[2 * experts], s] != 0)
    def _():
        for n in range(count):
            @pl.when(s == n)
            def _():
                buf[:keep] = h_refs[n][...]
        row = pl.multiple_of(live_ref[experts + e], ROW)
        rows = buf[pl.ds(row, acc.shape[1])]
        part = min(256, acc.shape[2]) if acc.shape[2] % 256 == 0 else 128

        @pl.loop(0, acc.shape[2] // part)
        def _(j):
            lanes = pl.ds(pl.multiple_of(j * part, part), part)
            acc[0, :, lanes] += jnp.dot(rows, w_ref[0, :, lanes], preferred_element_type=f32)


def plan_rows(choices, experts, experts_inner):
    def row(z):
        blocks = [choice(z) for choice in choices]
        valid = [int(b is not None) for b in blocks]
        some = [b for b in blocks if b is not None]
        at = (0, some[0] if some else 0)
        steps = (
            [(s, e) for s in range(len(blocks)) for e in range(experts)]
            if experts_inner
            else [(s, e) for e in range(experts) for s in range(len(blocks))]
        )
        held = []
        for s, e in steps:
            if blocks[s] is not None:
                at = (e, blocks[s])
            held.append(at)
        return valid + [a for a, _ in held] + [b for _, b in held]
    return row


def up_call(x2, weight, live, plan, slots, keep, width, after):
    experts, tiles, twice, deep = x2.shape
    tile = twice // 2
    steps = slots * experts

    def w_index(s, e, live_ref, plan_ref):
        z, at = live_ref[2 * experts], slots + s * experts + e
        return plan_ref[z, at], 0, 0, plan_ref[z, at + steps]

    return pl.pallas_call(
        functools.partial(up_kernel, experts, slots),
        grid_spec=pltpu.PrefetchScalarGridSpec(
            num_scalar_prefetch=2,
            grid=(slots, experts),
            in_specs=[
                pl.BlockSpec(x2.shape, lambda *_: (0, 0, 0, 0), pipeline_mode=pl.Buffered(1)),
                pl.BlockSpec((1, deep // 2, 2, width), w_index),
            ] + [pl.BlockSpec(memory_space=pl.ANY)] * len(after),
            out_specs=pl.BlockSpec((1, 2, keep + tile, width), lambda s, e, *_: (s, 0, 0, 0)),
            scratch_shapes=[pltpu.VMEM((deep, width), bf16)],
        ),
        out_shape=jax.ShapeDtypeStruct((slots, 2, keep + tile, width), bf16),
        compiler_params=pltpu.CompilerParams(vmem_limit_bytes=VMEM_LIMIT),
        cost_estimate=pl.CostEstimate(
            flops=2 * steps * tiles * twice * deep * width,
            bytes_accessed=2 * steps * deep * width + 2 * x2.size,
            transcendentals=0,
        ),
    )(live, plan, x2, weight, *after)


def down_call(h_list, weight, live, plan, acc, cap):
    experts, _, wide = weight.shape
    count = len(h_list)
    keep, fb = h_list[0].shape
    steps = count * experts

    def w_index(e, s, live_ref, plan_ref):
        z, at = live_ref[2 * experts], count + e * count + s
        return plan_ref[z, at], plan_ref[z, at + steps], 0

    acc_spec = pl.BlockSpec((1, cap, wide), lambda e, s, *_: (e, 0, 0))
    return pl.pallas_call(
        functools.partial(down_kernel, experts, count, acc is not None),
        grid_spec=pltpu.PrefetchScalarGridSpec(
            num_scalar_prefetch=2,
            grid=(experts, count),
            in_specs=[pl.BlockSpec((keep, fb), lambda *_: (0, 0))] * count
            + [pl.BlockSpec((1, fb, wide), w_index)]
            + ([acc_spec] if acc is not None else []),
            out_specs=acc_spec,
            scratch_shapes=[pltpu.VMEM((experts * cap, fb), bf16)],
        ),
        out_shape=jax.ShapeDtypeStruct((experts, cap, wide), f32),
        compiler_params=pltpu.CompilerParams(vmem_limit_bytes=VMEM_LIMIT),
        cost_estimate=pl.CostEstimate(
            flops=2 * steps * cap * fb * wide,
            bytes_accessed=2 * steps * fb * wide + 8 * experts * cap * wide,
            transcendentals=0,
        ),
    )(live, plan, *h_list, weight, *([acc] if acc is not None else []))


def experts_on(keep, n, pieces, cap, tile, x2, live, weight_up, weight_down):
    experts = weight_up.shape[0]
    fb = weight_up.shape[-1] // n // pieces
    right = [(d, d + 1) for d in range(n - 1)]
    left = [(d + 1, d) for d in range(n - 1)]

    def plan_of(choices, experts_inner):
        row = plan_rows(choices, experts, experts_inner)
        return jnp.asarray(np.array([row(d) for d in range(n)], np.int32))

    def within(block, k, holds):
        return block * pieces + k if holds else None

    def shift(value, pairs):
        return lax.ppermute(value, "width", pairs)

    def to_right(k, t):
        return lambda d: within(d + n - 1 - t, k, d <= t and d < n - 1)

    def to_left(k, t):
        return lambda d: within(d - n + 1 + t, k, d >= n - 1 - t and d > 0)

    def at_home(k):
        return lambda d: within(d, k, True)

    def terms(k, first, last, home, *after):
        choices = []
        for t in range(first, last):
            choices += [to_right(k, t), to_left(k, t)]
        choices += [at_home(k)] * home
        if not choices:
            return []
        out = up_call(x2, weight_up, live, plan_of(choices, True), len(choices), keep, fb, after)
        return [out[i, :, :keep] for i in range(len(choices))]

    def plus(got, term):
        return (got.astype(f32) + term.astype(f32)).astype(bf16)

    def down(held, choices, acc):
        if not held:
            return acc
        return down_call(held, weight_down, live, plan_of(choices, False), acc, cap)

    def send(k, t, part, got):
        right_sum, left_sum = part
        if t:
            right_sum, left_sum = plus(got[0], right_sum), plus(got[1], left_sum)
        sent[k, t] = right_sum
        return (
            shift(right_sum, [p for p in right if p[0] <= t]),
            shift(left_sum, [p for p in left if p[0] >= n - 1 - t]),
        )

    sent, got, parts = {}, {}, {}
    for k in range(pieces):
        follows = [sent[k - 1, min(1, n - 2)]] if k and n > 1 else []
        parts[k] = terms(k, 0, min(1, n - 1), False, *follows)
        if n > 1:
            got[k] = send(k, 0, parts[k], None)
            follows = [parts[k][0]]
            if k:
                follows.append(sent[k - 1, n - 2])
        parts[k] += terms(k, 1, n - 1, True, *follows)
        for t in range(1, n - 1):
            got[k] = send(k, t, parts[k][2 * t:2 * t + 2], got[k])

    acc = None
    late = []
    for k in range(pieces):
        home = parts[k][-1]
        if acc is not None:
            home, acc = lax.optimization_barrier((home, acc))
        both = home.astype(f32)
        if n > 1:
            both = both + got[k][0].astype(f32) + got[k][1].astype(f32)
        hidden = (jax.nn.silu(both[0]) * both[1]).astype(bf16)
        held, choices = [hidden], [at_home(k)]
        go_r = go_l = hidden
        for t in range(n - 1):
            if t == 1 and late:
                acc = down(*late.pop(), acc)
                go_r, acc = lax.optimization_barrier((go_r, acc))
            if t == 2:
                acc = down(held[:3], choices[:3], acc)
                if k == pieces - 1:
                    go_r, acc = lax.optimization_barrier((go_r, acc))
            go_r = shift(go_r, [p for p in right if p[0] >= t])
            go_l = shift(go_l, [p for p in left if p[0] <= n - 1 - t])
            held += [go_r, go_l]
            choices += [
                lambda d, t=t, k=k: within(d - 1 - t, k, d - 1 - t >= 0),
                lambda d, t=t, k=k: within(d + 1 + t, k, d + 1 + t < n),
            ]
        if n < 4:
            acc = down(held[:3], choices[:3], acc)
        late.append((held[3:], choices[3:]))
    for held, choices in late:
        for s in range(0, len(held), 2):
            acc = down(held[s:s + 2], choices[s:s + 2], acc)
    return acc


def local(n_width, n_hidden, tokens, expert_ids, skip_mask, pair_logits, gate_up_weight, down_weight):
    experts = gate_up_weight.shape[0]
    rows, depth = tokens.shape
    cores = 2 if n_hidden % 2 == 0 else 1
    chips = n_hidden // cores
    cap = MOST_DEV * n_hidden
    tile = min(128, cap)
    total = rows * n_hidden

    first = jax.nn.sigmoid(pair_logits[:, 0] - pair_logits[:, 1])
    second = jax.nn.sigmoid(pair_logits[:, 1] - pair_logits[:, 0])
    lanes = []
    scales = []
    for e in range(experts):
        hit_first = expert_ids[:, 0] == e
        hit_second = (expert_ids[:, 1] == e) & (skip_mask == 0)
        lanes.append((hit_first | hit_second).astype(f32))
        scales.append(jnp.where(hit_first, first, jnp.where(hit_second, second, 0.0)))
    for scale in scales:
        for _ in range(3):
            part = lax.reduce_precision(scale, 8, 7)
            lanes.append(part)
            scale = scale - part
    flags = jnp.stack(lanes, axis=1)
    flags = jnp.pad(flags, ((0, 0), (0, FLAGS - flags.shape[1]))).astype(bf16)

    swap = [(h, h ^ 1) for h in range(n_hidden)]

    def gather(value):
        blocks = [value]
        for dx in range(1, chips):
            blocks.append(lax.ppermute(value, "hidden", [
                ((x + dx) % chips * cores + c, x * cores + c)
                for x in range(chips) for c in range(cores)
            ]))
        value = jnp.concatenate(blocks, axis=0)
        if cores == 2:
            value = jnp.concatenate([value, lax.ppermute(value, "hidden", swap)], axis=0)
        return value

    flags = gather(flags).astype(f32)
    mine = gather(tokens)
    alive = flags[:, :experts]
    scale = flags[:, experts:4 * experts].reshape(total, experts, 3).sum(-1)
    tri = jnp.tril(jnp.ones((total, total), bf16))
    rank = jnp.dot(tri, alive.astype(bf16), preferred_element_type=f32).astype(i32) - 1
    slot = jnp.where(alive > 0, rank, -1)
    select = slot.T[:, None, :] == jnp.arange(cap, dtype=i32)[None, :, None]
    count = rank[-1] + 1
    offset = [jnp.zeros((), i32)]
    for e in range(experts):
        offset.append(offset[-1] + up_to(count[e], ROW))
    live = jnp.concatenate([count, jnp.stack([*offset[:-1], lax.axis_index("width")])])
    slot_scale = jnp.where(select, scale.T[:, None, :], 0.0).sum(-1)

    block = 256 if depth % 256 == 0 else 128
    spread = np.zeros((2, block, 2 * block), np.float32)
    for g in range(2):
        spread[g, np.arange(block), 2 * np.arange(block) + g] = 1
    picker = select.astype(bf16)
    x2 = pl.pallas_call(
        pack_kernel,
        grid=(depth // block,),
        in_specs=[
            pl.BlockSpec(picker.shape, lambda k: (0, 0, 0)),
            pl.BlockSpec((total, block), lambda k: (0, k)),
            pl.BlockSpec(spread.shape, lambda k: (0, 0, 0)),
        ],
        out_specs=pl.BlockSpec((experts, cap // tile, 2 * tile, 2 * block), lambda k: (0, 0, 0, k)),
        out_shape=jax.ShapeDtypeStruct((experts, cap // tile, 2 * tile, 2 * depth), bf16),
        compiler_params=pltpu.CompilerParams(vmem_limit_bytes=VMEM_LIMIT),
    )(picker, mine, jnp.asarray(spread, bf16))

    own_hidden = gate_up_weight.shape[-1] // n_width
    pieces = max(1, min(2, own_hidden // 128))
    most = experts * cap
    sizes = sorted({min(most, up_to(most * part // 32, ROW)) for part in (17, 21, 32)})
    run = [
        functools.partial(experts_on, keep, n_width, pieces, cap, tile) for keep in sizes
    ]
    need = offset[-2] + count[-1]
    which = sum((need > keep).astype(i32) for keep in sizes[:-1])
    out = lax.switch(which, run, x2, live, gate_up_weight, down_weight)

    used = jnp.arange(cap, dtype=i32)[None, :, None] < count[:, None, None]
    scaled = jnp.where(used, out * slot_scale[:, :, None], 0.0)
    high = lax.reduce_precision(scaled, 8, 7)
    low = (scaled - high).astype(bf16)
    term = functools.partial(jnp.einsum, "est,esd->td", preferred_element_type=f32)
    mixed = term(picker, high.astype(bf16)) + term(picker, low)
    if cores == 2:
        half = total // 2
        mixed = mixed[:half] + lax.ppermute(mixed[half:].astype(bf16), "hidden", swap).astype(f32)
    result = mixed[:rows]
    for dx in range(1, chips):
        piece = mixed[dx * rows:(dx + 1) * rows].astype(bf16)
        result = result + lax.ppermute(piece, "hidden", [
            (x * cores + c, (x + dx) % chips * cores + c) for x in range(chips) for c in range(cores)
        ]).astype(f32)
    return result.astype(bf16)


def solution(mesh):
    placed = (
        P(("groups", "hidden"), "width"),
        P(("groups", "hidden"), None),
        P(("groups", "hidden")),
        P(("groups", "hidden"), None),
        P(None, "width", None, "hidden"),
        P(None, "hidden", "width"),
    )
    return jax.shard_map(
        functools.partial(local, mesh.shape["width"], mesh.shape["hidden"]),
        mesh=mesh,
        in_specs=placed,
        out_specs=P(("groups", "hidden"), "width"),
        check_vma=False,
    )
```
